32 devices in a mesh: seq: 8 (over z, x), type: 4 (over y, core).
Axes of the slice: x: 2, y: 2, z: 4, core: 2. Of those that a mesh axis runs over, the one named last changes fastest.
Arguments:
- tokens: bfloat16 [4352, 1024], P(('seq', 'type')), may hold values from -60 to 60
- shift_scale: float32 [2, 1024], replicated, may hold values from -0.8 to 0.8
- branch_gate: float32 [1024], replicated, may hold values from 0.25 to 1.75
- final_gain: float32 [1024], replicated, may hold values from 0.5 to 1.5
- w_qkv: bfloat16 [3, 1024, 1024], P(None, None, 'type'), may hold values from -1 to 1
- w_out: bfloat16 [1024, 1024], P('type'), may hold values from -0.375 to 0.375
- type_ids: int32 [4352, 1], P(('seq', 'type')), may hold values from 0 to 7; in each aligned block of 136 rows (0 to 135, 136 to 271, ...) at most 51 rows name the same one
- head_w1: bfloat16 [8, 1024, 1024], P('type'), may hold values from -0.1875 to 0.1875
- head_b1: bfloat16 [8, 1024], P('type'), may hold values from -3 to 3
- head_w2: bfloat16 [8, 1024, 16], P('type'), may hold values from -0.1875 to 0.1875
Outputs:
- updated: bfloat16 [4352, 1024], P(('seq', 'type'))
- head_out: float32 [4352, 16], P(('seq', 'type'))
The draws below stay inside these ranges and needn't reach their ends.
Inputs may be any that keep to these rules, and one draw needn't show every extreme that they name: `type_ids`: among the 136 tokens of one device no type occurs more than 51 times; some type occurs exactly 51 times on some devices.
All inputs are finite; a program needn't handle non-finite values.
Results may differ from the reference program's by a relative error of at most 0.014.
Values may be sent and summed in bfloat16 or wider, within the bound.
A program may use at most 192 MiB of HBM per device.

```python
import math
import jax
import jax.numpy as jnp
import numpy as np
from jax import lax

D = 1024
HEADS = 16
HD = 64
HH = 1024
OUTS = 16
TOK_DEV = 136
TOKENS = 4352
NTYPES = 8
CAP = 51


def draw_tokens(key, part):
    groups = TOKENS // 8
    members = jax.random.randint(jax.random.fold_in(key, 6), (TOKENS,), 0, groups)
    row_scales = jnp.exp(jax.random.uniform(jax.random.fold_in(key, 1), (TOKENS, 1), jnp.float32, jnp.log(0.3), jnp.log(3.0)))
    col_scales = jnp.exp(jax.random.uniform(jax.random.fold_in(key, 2), (1, D), jnp.float32, jnp.log(0.3), jnp.log(3.0)))
    centers = jax.random.normal(jax.random.fold_in(key, 3), (groups, D), jnp.float32)
    jitter = jax.random.normal(jax.random.fold_in(key, 4), (TOKENS, D), jnp.float32)
    blended = 0.95 * centers[members] + 0.32 * jitter
    values = blended * row_scales * col_scales
    values = 0.25 * values
    return jnp.clip(values, -60.0, 60.0).astype(jnp.bfloat16)


def draw_w_qkv(key, part):
    query_spread = 2.0 / D ** 0.5
    value_spread = 1.0 / D ** 0.5
    basis = jax.random.normal(jax.random.fold_in(key, 5), (3, D, HEADS * HD), jnp.float32)
    basis = jnp.clip(basis, -6.0, 6.0)
    query_part = basis[0] * query_spread
    key_part = (0.4 * basis[0] + 0.5 * basis[1]) * query_spread
    value_part = basis[2] * value_spread
    values = jnp.stack([query_part, key_part, value_part], axis=0)
    return jnp.clip(values, -1.0, 1.0).astype(jnp.bfloat16)


def block_scale(key, dims, cuts, smallest, high):
    loudness, own = 1.0, jax.random.fold_in(key, 6)
    for dim, shards_of in cuts:
        steps = jnp.exp(jax.random.uniform(jax.random.fold_in(own, dim), (shards_of,), jnp.float32, smallest / len(cuts), high / len(cuts)))
        loudness = loudness * jnp.repeat(steps, dims[dim] // shards_of).reshape([-1 if axis == dim else 1 for axis in range(len(dims))])
    return loudness


def shared_out(key, own, number, rows, number_of, top, bound, slope):
    sequence = jax.random.permutation(key, number_of)
    packed, ordinary = shares(number_of, rows * top, bound, slope, True), shares(number_of, rows * top, bound, slope, False)
    places = jnp.arange(number_of)

    def named(tallies, rotation):
        used = int((tallies > 0).sum())
        fixed = max(1, used // 4)
        shifted = fixed + (places - fixed + rotation * (used - fixed)) % max(1, number_of - fixed)
        return jnp.zeros((number_of,), jnp.int32).at[sequence[jnp.where(places < fixed, places, shifted)]].set(jnp.asarray(tallies, jnp.int32))

    tallies = jnp.where(number % 4 == 0, named(packed, number // 4), named(ordinary, number - number // 4 - 1))
    mixed = jax.random.permutation(jax.random.fold_in(own, 3), number_of)
    source_of, taker = mixed[0:number_of // 2 * 2:2], mixed[1:number_of // 2 * 2:2]
    room = jnp.minimum(tallies[source_of] - 1, bound - tallies[taker]) // 2
    room = jnp.where((source_of == sequence[0]) | (taker == sequence[0]) | (tallies[taker] == 0), 0, jnp.maximum(room, 0))
    shifted = jax.random.randint(jax.random.fold_in(own, 4), (number_of // 2,), 0, 1 << 20) % (room + 1)
    tallies = tallies.at[source_of].add(-shifted).at[taker].add(shifted)
    items = jnp.searchsorted(jnp.cumsum(tallies), jnp.arange(rows * top), side="right").astype(jnp.int32)
    listing = items.reshape(top, rows).T
    listing = listing[jax.random.permutation(jax.random.fold_in(own, 1), rows)]
    rotation = jax.random.randint(jax.random.fold_in(own, 2), (rows, 1), 0, top)
    return jnp.take_along_axis(listing, (jnp.arange(top)[None, :] + rotation) % top, axis=1)


def shares(number_of, total, reach, lean, full):
    loads = [(1 << 20) // math.isqrt(rank ** lean) + 1 for rank in range(1, number_of + 1)]
    largest = reach if full else min(reach, max(-(-total // number_of), total * loads[0] // sum(loads)))
    least = 1 if total - largest >= number_of - 1 else 0
    given, surplus = [largest] + [least] * (number_of - 1), total - largest - least * (number_of - 1)
    while surplus > 0:
        free = [i for i in range(1, number_of) if given[i] < largest] or [i for i in range(1, number_of) if given[i] < reach]
        pool, remaining = sum([loads[i] for i in free]), surplus
        for i in free:
            addition = min(reach - given[i], max(1, remaining * loads[i] // pool), surplus)
            given[i] = given[i] + addition
            surplus = surplus - addition
    return np.array(given)


def gaussian(rng, shape, width, reach, cuts=(), held_as=jnp.bfloat16):
    entries = width * jax.random.normal(rng, shape, jnp.float32)
    if cuts:
        entries = entries * block_scale(rng, shape, cuts, -0.22, 0.18)
    return jnp.clip(entries, -reach, reach).astype(held_as)


def setup_inputs(seed: int = 0) -> dict:
    keys = jax.random.split(jax.random.key(seed), 11)
    tokens = draw_tokens(jax.random.fold_in(keys[10], 71), 0)
    shift_scale = gaussian(keys[1], (2, D), 0.2, 0.8, (), jnp.float32)
    branch_gate = jnp.clip(1.0 + 0.15 * jax.random.normal(keys[2], (D,), jnp.float32), 0.25, 1.75)
    final_gain = jnp.clip(1.0 + 0.1 * jax.random.normal(keys[3], (D,), jnp.float32), 0.5, 1.5)
    w_qkv = draw_w_qkv(jax.random.fold_in(keys[10], 71), 0)
    w_out = gaussian(keys[5], (HEADS * HD, D), (HEADS * HD // 4) ** -0.5, 0.375, ((0, 4),))
    type_ids_keys = jax.random.split(jax.random.fold_in(keys[6], 1), TOKENS // TOK_DEV)
    type_ids_turns = jax.random.permutation(jax.random.fold_in(keys[6], 3), TOKENS // TOK_DEV)
    type_ids = jax.vmap(lambda own, number: shared_out(jax.random.fold_in(keys[6], 2), own, number, TOK_DEV, NTYPES, 1, CAP, 2))(type_ids_keys, type_ids_turns).reshape((TOKENS, 1))
    head_w1 = gaussian(keys[7], (NTYPES, D, HH), D ** -0.5, 0.1875, ((0, 4),))
    head_b1 = gaussian(keys[8], (NTYPES, HH), 0.5, 3.0, ((0, 4),))
    head_w2 = gaussian(keys[9], (NTYPES, HH, OUTS), HH ** -0.5, 0.1875, ((0, 4),))
    return {"tokens": tokens, "shift_scale": shift_scale, "branch_gate": branch_gate, "final_gain": final_gain, "w_qkv": w_qkv, "w_out": w_out, "type_ids": type_ids, "head_w1": head_w1, "head_b1": head_b1, "head_w2": head_w2}


def rms_normalize(values):
    squares = lax.optimization_barrier(jnp.mean(values * values, axis=-1, keepdims=True))
    return values * lax.rsqrt(squares + 1e-06)

def reference(tokens, shift_scale, branch_gate, final_gain, w_qkv, w_out, type_ids, head_w1, head_b1, head_w2):
    inputs = tokens.astype(jnp.float32)
    modulated = (rms_normalize(inputs) * (1.0 + shift_scale[1]) + shift_scale[0]).astype(jnp.bfloat16)
    projected = [jnp.dot(modulated.astype(jnp.float32), w_qkv[which].astype(jnp.float32), preferred_element_type=jnp.float32).astype(jnp.bfloat16) for which in range(3)]
    queries = projected[0].astype(jnp.float32).reshape(TOKENS, HEADS, HD)
    all_keys = projected[1].astype(jnp.float32).reshape(TOKENS, HEADS, HD)
    all_values = projected[2].astype(jnp.float32).reshape(TOKENS, HEADS, HD)
    factor = HD ** (-0.5)

    def attend(query_block):
        scores = jnp.einsum('qhd,khd->hqk', query_block, all_keys) * factor
        largest = lax.optimization_barrier(jnp.max(scores, axis=-1, keepdims=True))
        weights = jnp.exp(scores - largest)
        totals = lax.optimization_barrier(jnp.sum(weights, axis=-1))
        rounded = lax.optimization_barrier(weights.astype(jnp.bfloat16)).astype(jnp.float32)
        numer = jnp.einsum('hqk,khd->qhd', rounded, all_values)
        return (numer / jnp.transpose(totals)[:, :, None]).astype(jnp.bfloat16)
    block_rows = min(256, TOKENS)
    attended = lax.map(attend, queries.reshape(TOKENS // block_rows, block_rows, HEADS, HD))
    attended = attended.reshape(TOKENS, HEADS * HD)
    mixed = jnp.dot(attended.astype(jnp.float32), w_out.astype(jnp.float32), preferred_element_type=jnp.float32)
    updated = (inputs + branch_gate * mixed).astype(jnp.bfloat16)
    final = (rms_normalize(updated.astype(jnp.float32)) * final_gain).astype(jnp.bfloat16)
    kinds = type_ids[:, 0]
    head_out = jnp.zeros((TOKENS, OUTS), jnp.float32)
    for kind in range(NTYPES):
        hidden = jax.nn.gelu(jnp.dot(final.astype(jnp.float32), head_w1[kind].astype(jnp.float32), preferred_element_type=jnp.float32) + head_b1[kind].astype(jnp.float32)).astype(jnp.bfloat16)
        result = jnp.dot(hidden.astype(jnp.float32), head_w2[kind].astype(jnp.float32), preferred_element_type=jnp.float32)
        head_out = jnp.where((kinds == kind)[:, None], result, head_out)
    return (updated, head_out)
```

```python
import functools

import jax
import jax.numpy as jnp
from jax import lax
from jax.experimental import pallas as pl
from jax.experimental.pallas import tpu as pltpu
from jax.sharding import PartitionSpec as P

HD = 64
MESH = pl.DeviceIdType.MESH
F32 = jnp.float32
BF16 = jnp.bfloat16


def rms_normalize(values):
    squares = jnp.mean(values * values, axis=-1, keepdims=True)
    return values * lax.rsqrt(squares + 1e-06)


def greet(peers):
    barrier = pltpu.get_barrier_semaphore()
    for peer in peers:
        pl.semaphore_signal(barrier, inc=1, device_id=peer, device_id_type=MESH)
    pl.semaphore_wait(barrier, len(peers))


def remote(src, dst, send, recv, peer):
    return pltpu.make_async_remote_copy(
        src_ref=src, dst_ref=dst, send_sem=send, recv_sem=recv, device_id=peer, device_id_type=MESH
    )


def partners(t):
    core = t + 1 - 2 * (t % 2)
    across = (t + 2) % 4
    diag = core + 2 - 4 * (core // 2)
    return core, across, diag


def project_kernel(
    S, HL, tok, ss, wqkv, wout, q_out, kv_out, wf_out,
    mod, proj, qsend, kvsend, m_s, m_r, w_s, w_r, q_s, q_r, k_s, k_r, f_s, f_r, l_s,
):
    G = S // HL
    s = lax.axis_index("seq")
    t = lax.axis_index("type")
    h0, g = s // G, s % G
    core, across, diag = partners(t)
    zs = [((h0 + d) % HL) * G + g for d in range(HL)]
    froms = [((h0 + HL - d) % HL) * G + g for d in range(HL)]
    groups = [h0 * G + (g + e) % G for e in range(G)]
    greet(
        [(s, core), (s, across)]
        + [(zs[d], t) for d in range(1, HL)]
        + [(groups[e], t) for e in range(1, G)]
    )
    x = tok[...].astype(F32)
    mod[t] = (rms_normalize(x) * (1.0 + ss[1:2]) + ss[0:1]).astype(BF16)
    to_across = remote(mod.at[t], mod.at[t], m_s.at[1], m_r.at[1], (s, across))
    to_across.start()
    to_core = remote(mod.at[t], mod.at[t], m_s.at[0], m_r.at[0], (s, core))
    to_core.start()

    def project(i):
        block = mod[i]
        for which in range(3):
            proj[i, :, which * 256 : which * 256 + 256] = jnp.dot(
                block, wqkv[which], preferred_element_type=F32
            )

    own_w = pltpu.make_async_copy(wout, wf_out.at[t], l_s.at[0])
    own_w.start()
    project(t)
    remote(mod.at[core], mod.at[core], m_s.at[0], m_r.at[0], (s, core)).wait_recv()
    project(core)
    remote(mod.at[across], mod.at[across], m_s.at[1], m_r.at[1], (s, across)).wait_recv()
    passed = remote(mod.at[across], mod.at[across], m_s.at[2], m_r.at[2], (s, core))
    passed.start()
    w_across = remote(wout, wf_out.at[t], w_s.at[1], w_r.at[1], (s, across))
    w_across.start()
    project(across)
    remote(mod.at[diag], mod.at[diag], m_s.at[2], m_r.at[2], (s, core)).wait_recv()
    project(diag)

    rows = proj.shape[0] * proj.shape[1]
    half = rows // 2
    for h in range(HL):
        k = proj[:, :, 256 + h * HD : 256 + h * HD + HD].reshape(rows, HD)
        v = proj[:, :, 512 + h * HD : 512 + h * HD + HD].reshape(rows, HD)
        kvsend[h] = jnp.concatenate([k, v], axis=-1).astype(BF16)
    sends = []
    for d in range(1, HL):
        hp = (h0 + d) % HL
        c = remote(kvsend.at[hp], kv_out.at[s], k_s.at[d], k_r.at[d], (zs[d], t))
        c.start()
        sends.append(c)
    own_kv = pltpu.make_async_copy(kvsend.at[h0], kv_out.at[s], l_s.at[1])
    own_kv.start()
    for e in range(1, G):
        c = remote(kvsend.at[h0], kv_out.at[s], f_s.at[0, e], f_r.at[0, e], (groups[e], t))
        c.start()
        sends.append(c)
    for h in range(HL):
        q = proj[:, :, h * HD : h * HD + HD].reshape(rows, HD)
        qsend[h] = jnp.concatenate([q[:half], q[half:]], axis=-1).astype(BF16)
    for d in range(1, HL):
        hp = (h0 + d) % HL
        c = remote(qsend.at[hp], q_out.at[h0], q_s.at[d], q_r.at[d], (zs[d], t))
        c.start()
        sends.append(c)
    own_q = pltpu.make_async_copy(qsend.at[h0], q_out.at[h0], l_s.at[2])
    own_q.start()
    w_core = remote(wout, wf_out.at[t], w_s.at[0], w_r.at[0], (s, core))
    w_core.start()

    for d in range(1, HL):
        slot = kv_out.at[froms[d]]
        remote(slot, slot, k_s.at[d], k_r.at[d], (zs[d], t)).wait_recv()
        for e in range(1, G):
            c = remote(slot, slot, f_s.at[d, e], f_r.at[d, e], (groups[e], t))
            c.start()
            sends.append(c)
    slot = wf_out.at[across]
    remote(slot, slot, w_s.at[1], w_r.at[1], (s, across)).wait_recv()
    w_passed = remote(slot, slot, w_s.at[2], w_r.at[2], (s, core))
    w_passed.start()

    for d in range(1, HL):
        slot = q_out.at[(h0 + HL - d) % HL]
        remote(slot, slot, q_s.at[d], q_r.at[d], (zs[d], t)).wait_recv()
    for d in range(HL):
        for e in range(1, G):
            slot = kv_out.at[((h0 + HL - d) % HL) * G + (g + G - e) % G]
            remote(slot, slot, f_s.at[d, e], f_r.at[d, e], (groups[e], t)).wait_recv()
    slot = wf_out.at[core]
    remote(slot, slot, w_s.at[0], w_r.at[0], (s, core)).wait_recv()
    slot = wf_out.at[diag]
    remote(slot, slot, w_s.at[2], w_r.at[2], (s, core)).wait_recv()
    for c in [to_across, to_core, passed, w_across, w_core, w_passed] + sends:
        c.wait_send()
    own_w.wait()
    own_kv.wait()
    own_q.wait()


def attend_kernel(chunk, q_ref, kv_ref, out_ref, vv, numer, top):
    keys = kv_ref.shape[0]

    @pl.when(pl.program_id(0) == 0)
    def _():
        kv = kv_ref[...]
        lane = lax.broadcasted_iota(jnp.int32, kv.shape, 1)
        vv[...] = jnp.where(lane < HD, jnp.ones_like(kv), kv)

    packed = q_ref[...]
    rows = packed.shape[0]
    zeros = jnp.zeros((rows, HD), BF16)
    factor = HD ** (-0.5)
    for half in range(2):
        q = jnp.concatenate([packed[:, half * HD : half * HD + HD], zeros], axis=-1)

        def scores_of(lo):
            return lax.dot_general(
                q, kv_ref[pl.ds(lo, chunk), :], (((1,), (1,)), ((), ())), preferred_element_type=F32
            )

        if keys == chunk:
            sc = scores_of(0)
            m = jnp.max(sc, axis=-1, keepdims=True)
            p = jnp.exp((sc - m) * factor).astype(BF16)
            o = jnp.dot(p, vv[...], preferred_element_type=F32)
        else:
            numer[...] = jnp.zeros_like(numer)
            top[...] = jnp.full_like(top, -1e30)

            def step(i, carry):
                lo = pl.multiple_of(i * chunk, chunk)
                sc = scores_of(lo)
                old = top[...]
                m = jnp.maximum(old, jnp.max(sc, axis=-1, keepdims=True))
                p = jnp.exp((sc - m) * factor).astype(BF16)
                numer[...] = numer[...] * jnp.exp((old - m) * factor) + jnp.dot(
                    p, vv[pl.ds(lo, chunk), :], preferred_element_type=F32
                )
                top[...] = m
                return carry

            lax.fori_loop(0, keys // chunk, step, 0)
            o = numer[...]
        a = o[:, HD:] / o[:, :HD]
        block = rows // 2
        for j in range(2):
            b = a[j * block : (j + 1) * block]
            out_ref[half * 2 + j] = jnp.concatenate(
                [b[0:80], b[block - 80 : block]], axis=-1
            ).astype(BF16)


def finish_kernel(
    S, HL, T, att_send, wf, tok, gate, gain, kinds, w1, b1, w2,
    upd_out, head_out,
    arecv, att, fin, rsend, rrecv, a_s, a_r, m_s, m_r, r_s, r_r, l_s,
):
    G = S // HL
    s = lax.axis_index("seq")
    t = lax.axis_index("type")
    h0, g = s // G, s % G
    core, across, diag = partners(t)
    P0 = h0 * T + t
    N = HL * T

    def device(p):
        return ((p // T) * G + g, p % T)

    peers = [(P0 + d) % N for d in range(N)]
    froms = [(P0 + N - d) % N for d in range(N)]
    greet([device(peers[d]) for d in range(1, N)])
    mine = t * HL + h0
    sends = []
    for d in range(1, N):
        c = remote(att_send.at[peers[d]], arecv.at[mine], a_s.at[d], a_r.at[d], device(peers[d]))
        c.start()
        sends.append(c)
    own = pltpu.make_async_copy(att_send.at[P0], arecv.at[mine], l_s.at[0])
    own.start()
    own.wait()
    for d in range(1, N):
        slot = arecv.at[(froms[d] % T) * HL + froms[d] // T]
        remote(slot, slot, a_s.at[d], a_r.at[d], device(peers[d])).wait_recv()
    block = tok.shape[0]
    for j in range(N // 2):
        pair = []
        for i in (2 * j, 2 * j + 1):
            r = arecv[i].astype(F32)
            pair.append(jnp.concatenate([r[:, :HD], r[160 - block : 80, HD:]], axis=0))
        att[:, 128 * j : 128 * j + 128] = jnp.concatenate(pair, axis=-1).astype(BF16)
    mixed = jnp.dot(att[...], wf[...], preferred_element_type=F32)
    updated = (tok[...].astype(F32) + gate[...] * mixed).astype(BF16)
    upd_out[...] = updated
    fin[t] = (rms_normalize(updated.astype(F32)) * gain[...]).astype(BF16)
    to_across = remote(fin.at[t], fin.at[t], m_s.at[1], m_r.at[1], (s, across))
    to_across.start()
    to_core = remote(fin.at[t], fin.at[t], m_s.at[0], m_r.at[0], (s, core))
    to_core.start()

    def heads(i, dst):
        f = fin[i]
        for k in range(2):
            hid = jnp.dot(f, w1[k], preferred_element_type=F32) + b1[k : k + 1].astype(F32)
            hid = jax.nn.gelu(hid).astype(BF16)
            dst[k * 16 : k * 16 + 16, :] = lax.dot_general(
                w2[k], hid, (((1,), (1,)), ((), ())), preferred_element_type=F32
            )

    heads(t, rrecv.at[t])
    remote(fin.at[core], fin.at[core], m_s.at[0], m_r.at[0], (s, core)).wait_recv()
    heads(core, rsend.at[0])
    c = remote(rsend.at[0], rrecv.at[t], r_s.at[0], r_r.at[0], (s, core))
    c.start()
    sends.append(c)
    remote(fin.at[across], fin.at[across], m_s.at[1], m_r.at[1], (s, across)).wait_recv()
    passed = remote(fin.at[across], fin.at[across], m_s.at[2], m_r.at[2], (s, core))
    passed.start()
    heads(across, rsend.at[1])
    c = remote(rsend.at[1], rrecv.at[t], r_s.at[1], r_r.at[1], (s, across))
    c.start()
    sends.append(c)
    remote(fin.at[diag], fin.at[diag], m_s.at[2], m_r.at[2], (s, core)).wait_recv()
    heads(diag, rsend.at[2])
    c = remote(rsend.at[2], rrecv.at[t], r_s.at[2], r_r.at[2], (s, diag))
    c.start()
    sends.append(c)
    for i, peer in enumerate((core, across, diag)):
        slot = rrecv.at[peer]
        remote(slot, slot, r_s.at[i], r_r.at[i], (s, peer)).wait_recv()
    kind = kinds[...]
    total = jnp.zeros((16, block), F32)
    for owner in range(T):
        for k in range(2):
            total = jnp.where(kind == 2 * owner + k, rrecv[owner, k * 16 : k * 16 + 16, :], total)
    head_out[...] = total
    for c in [to_across, to_core, passed] + sends:
        c.wait_send()


VM = pl.BlockSpec(memory_space=pltpu.VMEM)
HB = pl.BlockSpec(memory_space=pl.ANY)


def body(
    S, T,
    tokens, shift_scale, branch_gate, final_gain, w_qkv, w_out, type_ids, head_w1, head_b1, head_w2
):
    block, D = tokens.shape
    width = w_qkv.shape[2]
    HL = width // HD
    G = S // HL
    rows = block * T
    dma = pltpu.SemaphoreType.DMA
    q, kv, wf = pl.pallas_call(
        functools.partial(project_kernel, S, HL),
        out_shape=(
            jax.ShapeDtypeStruct((HL, rows // 2, 128), BF16),
            jax.ShapeDtypeStruct((S, rows, 128), BF16),
            jax.ShapeDtypeStruct((T, width, D), BF16),
        ),
        in_specs=[VM] * 4,
        out_specs=(HB, HB, HB),
        scratch_shapes=[
            pltpu.VMEM((T, block, D), BF16),
            pltpu.VMEM((T, block, 3 * width), F32),
            pltpu.VMEM((HL, rows // 2, 128), BF16),
            pltpu.VMEM((HL, rows, 128), BF16),
            dma((3,)), dma((3,)), dma((3,)), dma((3,)),
            dma((HL,)), dma((HL,)), dma((HL,)), dma((HL,)),
            dma((HL, G)), dma((HL, G)), dma((3,)),
        ],
        compiler_params=pltpu.CompilerParams(
            collective_id=0, has_side_effects=True, vmem_limit_bytes=40 * 2**20
        ),
        name="project",
    )(tokens, shift_scale, w_qkv, w_out)

    keys = S * rows
    chunk = 8 * rows
    att = pl.pallas_call(
        functools.partial(attend_kernel, chunk),
        grid=(HL,),
        out_shape=jax.ShapeDtypeStruct((HL * T, 80, 128), BF16),
        in_specs=[
            pl.BlockSpec((rows // 2, 128), lambda i: (i, 0)),
            pl.BlockSpec((keys, 128), lambda i: (0, 0)),
        ],
        out_specs=pl.BlockSpec((T, 80, 128), lambda i: (i, 0, 0)),
        scratch_shapes=[
            pltpu.VMEM((keys, 128), BF16),
            pltpu.VMEM((rows // 2, 128), F32),
            pltpu.VMEM((rows // 2, 1), F32),
        ],
        compiler_params=pltpu.CompilerParams(vmem_limit_bytes=56 * 2**20),
        name="attend",
    )(q.reshape(HL * (rows // 2), 128), kv.reshape(keys, 128))

    N = HL * T
    updated, heads = pl.pallas_call(
        functools.partial(finish_kernel, S, HL, T),
        out_shape=(
            jax.ShapeDtypeStruct((block, D), BF16),
            jax.ShapeDtypeStruct((16, block), F32),
        ),
        in_specs=[VM] * 9,
        out_specs=(VM, VM),
        scratch_shapes=[
            pltpu.VMEM((N, 80, 128), BF16),
            pltpu.VMEM((block, D), BF16),
            pltpu.VMEM((T, block, D), BF16),
            pltpu.VMEM((3, 32, block), F32),
            pltpu.VMEM((T, 32, block), F32),
            dma((N,)), dma((N,)), dma((3,)), dma((3,)), dma((3,)), dma((3,)), dma((1,)),
        ],
        compiler_params=pltpu.CompilerParams(
            collective_id=1, has_side_effects=True, vmem_limit_bytes=40 * 2**20
        ),
        name="finish",
    )(
        att, wf.reshape(T * width, D), tokens, branch_gate.reshape(1, D), final_gain.reshape(1, D),
        type_ids.reshape(1, block), head_w1, head_b1, jnp.transpose(head_w2, (0, 2, 1)),
    )
    return (updated, heads.T)


def solution(mesh):
    in_specs = (
        P(("seq", "type"), None),
        P(),
        P(),
        P(),
        P(None, None, "type"),
        P("type", None),
        P(("seq", "type"), None),
        P("type", None, None),
        P("type", None),
        P("type", None, None),
    )
    out_specs = (P(("seq", "type"), None), P(("seq", "type"), None))
    return jax.shard_map(
        functools.partial(body, mesh.shape["seq"], mesh.shape["type"]),
        mesh=mesh, in_specs=in_specs, out_specs=out_specs, check_vma=False,
    )
```

```python
import functools

import jax
import jax.numpy as jnp
from jax import lax
from jax.experimental import pallas as pl
from jax.experimental.pallas import tpu as pltpu
from jax.sharding import PartitionSpec as P

HD = 64
MESH = pl.DeviceIdType.MESH
F32 = jnp.float32
BF16 = jnp.bfloat16


def rms_normalize(values):
    squares = jnp.mean(values * values, axis=-1, keepdims=True)
    return values * lax.rsqrt(squares + 1e-06)


def greet(peers):
    barrier = pltpu.get_barrier_semaphore()
    for peer in peers:
        pl.semaphore_signal(barrier, inc=1, device_id=peer, device_id_type=MESH)
    pl.semaphore_wait(barrier, len(peers))


def remote(src, dst, send, recv, peer):
    return pltpu.make_async_remote_copy(
        src_ref=src, dst_ref=dst, send_sem=send, recv_sem=recv, device_id=peer, device_id_type=MESH
    )


def partners(t):
    core = t + 1 - 2 * (t % 2)
    across = (t + 2) % 4
    diag = core + 2 - 4 * (core // 2)
    return core, across, diag


def kernel(
    S, HL, T,
    tok, ss, wqkv, wout, gate, gain, kinds, w1, b1, w2,
    upd_out, head_out,
    wq, wf, w1v, mod, proj, qsend, kvsend, qrecv, kv, qpad, vv, numer, top,
    asend, arecv, att, fin, rsend, rrecv,
    m_s, m_r, w_s, w_r, q_s, q_r, k_s, k_r, f_s, f_r, a_s, a_r, n_s, n_r, r_s, r_r, l_s,
):
    G = S // HL
    N = HL * T
    s = lax.axis_index("seq")
    t = lax.axis_index("type")
    h0, g = s // G, s % G
    core, across, diag = partners(t)
    zs = [((h0 + d) % HL) * G + g for d in range(HL)]
    groups = [h0 * G + (g + e) % G for e in range(G)]
    back = [(h0 + HL - d) % HL for d in range(HL)]
    block = tok.shape[0]
    rows = T * block
    half = rows // 2

    load_q = pltpu.make_async_copy(wqkv, wq, l_s.at[0])
    load_q.start()
    load_o = pltpu.make_async_copy(wout, wf.at[t], l_s.at[1])
    load_o.start()
    load_1 = pltpu.make_async_copy(w1, w1v, l_s.at[2])
    load_1.start()

    def device(h, tt):
        return (h * G + g, tt)

    greet(
        [
            device((h0 + d) % HL, (t + c) % T)
            for d in range(HL) for c in range(T) if d or c
        ]
        + [(groups[e], t) for e in range(1, G)]
    )
    x = tok[...].astype(F32)
    mod[t] = (rms_normalize(x) * (1.0 + ss[1:2]) + ss[0:1]).astype(BF16)
    sends = []

    def send(src, dst, a, b, peer):
        c = remote(src, dst, a, b, peer)
        c.start()
        sends.append(c)

    def arrive(slot, a, b):
        remote(slot, slot, a, b, (s, core)).wait_recv()

    send(mod.at[t], mod.at[t], m_s.at[1], m_r.at[1], (s, across))
    send(mod.at[t], mod.at[t], m_s.at[0], m_r.at[0], (s, core))

    def project(i):
        value = mod[i]
        for which in range(3):
            proj[i, :, which * 256 : which * 256 + 256] = jnp.dot(
                value, wq[which], preferred_element_type=F32
            )

    load_q.wait()
    project(t)
    arrive(mod.at[core], m_s.at[0], m_r.at[0])
    project(core)
    arrive(mod.at[across], m_s.at[1], m_r.at[1])
    send(mod.at[across], mod.at[across], m_s.at[2], m_r.at[2], (s, core))
    send(wout, wf.at[t], w_s.at[1], w_r.at[1], (s, across))
    project(across)
    arrive(mod.at[diag], m_s.at[2], m_r.at[2])
    project(diag)

    for h in range(HL):
        q = proj[:, :, h * HD : h * HD + HD].reshape(rows, HD)
        qsend[h] = jnp.concatenate([q[:half], q[half:]], axis=-1).astype(BF16)
    for d in range(1, HL):
        hp = (h0 + d) % HL
        send(qsend.at[hp], qrecv.at[h0], q_s.at[d], q_r.at[d], (zs[d], t))
    own_q = pltpu.make_async_copy(qsend.at[h0], qrecv.at[h0], l_s.at[3])
    own_q.start()
    for h in range(HL):
        k = proj[:, :, 256 + h * HD : 256 + h * HD + HD].reshape(rows, HD)
        v = proj[:, :, 512 + h * HD : 512 + h * HD + HD].reshape(rows, HD)
        kvsend[h] = jnp.concatenate([k, v], axis=-1).astype(BF16)
    for e in range(1, G):
        send(kvsend.at[h0], kv.at[s], f_s.at[0, e], f_r.at[0, e], (groups[e], t))
    own_kv = pltpu.make_async_copy(kvsend.at[h0], kv.at[s], l_s.at[4])
    own_kv.start()
    for d in range(1, HL):
        hp = (h0 + d) % HL
        send(kvsend.at[hp], kv.at[s], k_s.at[d], k_r.at[d], (zs[d], t))
    send(wout, wf.at[t], w_s.at[0], w_r.at[0], (s, core))

    def unpack(h):
        value = qrecv[h]
        zeros = jnp.zeros((half, HD), BF16)
        qpad[h * 2] = jnp.concatenate([value[:, :HD], zeros], axis=-1)
        qpad[h * 2 + 1] = jnp.concatenate([value[:, HD:], zeros], axis=-1)

    own_q.wait()
    unpack(h0)
    for d in range(1, HL):
        arrive(qrecv.at[back[d]], q_s.at[d], q_r.at[d])
        unpack(back[d])
    own_kv.wait()

    factor = HD ** (-0.5) * 1.4426950408889634
    chunks = max(G // 2, 1)
    per = G // chunks

    def keys_of(d, j):
        return kv[pl.ds(back[d] * G + j * per, per)].reshape(per * rows, 128)

    def values(d, j):
        value = keys_of(d, j)
        lane = lax.broadcasted_iota(jnp.int32, value.shape, 1)
        vv[...] = jnp.where(lane < HD, jnp.ones_like(value), value)

    def pair(d, j, h, first):
        kc = keys_of(d, j)
        scores = [
            lax.dot_general(
                qpad[h * 2 + i], kc, (((1,), (1,)), ((), ())), preferred_element_type=F32
            )
            for i in range(2)
        ]
        for i in range(2):
            sc = scores[i]
            m = jnp.max(sc, axis=-1, keepdims=True)
            if not first:
                old = top[h * 2 + i]
                m = jnp.maximum(m, old)
            p = jnp.exp2((sc - m) * factor).astype(BF16)
            o = jnp.dot(p, vv[...], preferred_element_type=F32)
            if not first:
                o = o + numer[h * 2 + i] * jnp.exp2((old - m) * factor)
            numer[h * 2 + i] = o
            top[h * 2 + i] = m

    def absorb(d, first_h, count):
        first = d == 0 and chunks == 1

        def over_chunks(j, carry):
            values(d, j)

            def over(i, inner):
                pair(d, j, (first_h + i) % HL, first)
                return inner

            lax.fori_loop(0, count, over, 0)
            return carry

        if chunks == 1:
            over_chunks(0, 0)
        else:
            lax.fori_loop(0, chunks, over_chunks, 0)

    if chunks > 1:
        numer[...] = jnp.zeros_like(numer)
        top[...] = jnp.full_like(top, -1e30)

    def group_arrives(d):
        for e in range(1, G):
            arrive(kv.at[back[d] * G + (g + G - e) % G], f_s.at[d, e], f_r.at[d, e])

    def emit(h):
        parts = []
        for i in range(2):
            o = numer[h * 2 + i]
            a = o[:, HD:] / o[:, :HD]
            for j in range(2):
                b = a[j * block : (j + 1) * block]
                asend[h * T + i * 2 + j] = jnp.concatenate(
                    [b[0:80], b[block - 80 : block]], axis=-1
                ).astype(BF16)

    mine = t * HL + h0
    group_arrives(0)
    for d in range(HL - 1):
        absorb(d, h0, HL // 2)
        slot = kv.at[back[d + 1] * G + g]
        arrive(slot, k_s.at[d + 1], k_r.at[d + 1])
        for e in range(1, G):
            send(slot, slot, f_s.at[d + 1, e], f_r.at[d + 1, e], (groups[e], t))
        if d == 0:
            arrive(wf.at[across], w_s.at[1], w_r.at[1])
            send(wf.at[across], wf.at[across], w_s.at[2], w_r.at[2], (s, core))
        absorb(d, h0 + HL // 2, HL // 2)
        group_arrives(d + 1)
    for i in range(HL):
        d = (i + 1) % HL
        h = (h0 + d) % HL
        absorb(HL - 1, h, 1)
        emit(h)
        for c in range(T):
            if d or c:
                tt = (t + c) % T
                send(
                    asend.at[h * T + tt], arecv.at[mine], a_s.at[d, c], a_r.at[d, c],
                    device(h, tt),
                )
    own_a = pltpu.make_async_copy(asend.at[h0 * T + t], arecv.at[mine], l_s.at[5])
    own_a.start()
    arrive(wf.at[core], w_s.at[0], w_r.at[0])
    arrive(wf.at[diag], w_s.at[2], w_r.at[2])
    load_o.wait()
    own_a.wait()
    for i in range(HL):
        d = (i + 1) % HL
        for c in range(T):
            if d or c:
                arrive(arecv.at[((t + T - c) % T) * HL + back[d]], a_s.at[d, c], a_r.at[d, c])
    for j in range(N // 2):
        both = []
        for i in (2 * j, 2 * j + 1):
            r = arecv[i].astype(F32)
            both.append(jnp.concatenate([r[:, :HD], r[160 - block : 80, HD:]], axis=0))
        att[:, 128 * j : 128 * j + 128] = jnp.concatenate(both, axis=-1).astype(BF16)
    mixed = jnp.dot(
        att[...], wf[...].reshape(N * HD, tok.shape[1]), preferred_element_type=F32
    )
    updated = (tok[...].astype(F32) + gate[...] * mixed).astype(BF16)
    upd_out[...] = updated
    fin[t] = (rms_normalize(updated.astype(F32)) * gain[...]).astype(BF16)
    send(fin.at[t], fin.at[t], n_s.at[1], n_r.at[1], (s, across))
    send(fin.at[t], fin.at[t], n_s.at[0], n_r.at[0], (s, core))

    def heads(i, dst):
        f = fin[i]
        for k in range(2):
            hid = jnp.dot(f, w1v[k], preferred_element_type=F32) + b1[k : k + 1].astype(F32)
            hid = jax.nn.gelu(hid).astype(BF16)
            dst[k * 16 : k * 16 + 16, :] = lax.dot_general(
                w2[k], hid, (((1,), (1,)), ((), ())), preferred_element_type=F32
            )

    load_1.wait()
    heads(t, rrecv.at[t])
    arrive(fin.at[core], n_s.at[0], n_r.at[0])
    heads(core, rsend.at[0])
    send(rsend.at[0], rrecv.at[t], r_s.at[0], r_r.at[0], (s, core))
    arrive(fin.at[across], n_s.at[1], n_r.at[1])
    send(fin.at[across], fin.at[across], n_s.at[2], n_r.at[2], (s, core))
    heads(across, rsend.at[1])
    send(rsend.at[1], rrecv.at[t], r_s.at[1], r_r.at[1], (s, across))
    arrive(fin.at[diag], n_s.at[2], n_r.at[2])
    heads(diag, rsend.at[2])
    send(rsend.at[2], rrecv.at[t], r_s.at[2], r_r.at[2], (s, diag))
    for i, peer in enumerate((core, across, diag)):
        arrive(rrecv.at[peer], r_s.at[i], r_r.at[i])
    kind = kinds[...]
    total = jnp.zeros((16, block), F32)
    for owner in range(T):
        for k in range(2):
            total = jnp.where(kind == 2 * owner + k, rrecv[owner, k * 16 : k * 16 + 16, :], total)
    head_out[...] = total
    for c in sends:
        c.wait_send()


VM = pl.BlockSpec(memory_space=pltpu.VMEM)
HB = pl.BlockSpec(memory_space=pltpu.HBM)


def body(
    S, T,
    tokens, shift_scale, branch_gate, final_gain, w_qkv, w_out, type_ids, head_w1, head_b1, head_w2
):
    block, D = tokens.shape
    width = w_qkv.shape[2]
    HL = width // HD
    G = S // HL
    N = HL * T
    rows = block * T
    half = rows // 2
    per = min(G, 2)
    dma = pltpu.SemaphoreType.DMA
    updated, heads = pl.pallas_call(
        functools.partial(kernel, S, HL, T),
        out_shape=(
            jax.ShapeDtypeStruct((block, D), BF16),
            jax.ShapeDtypeStruct((16, block), F32),
        ),
        in_specs=[VM, VM, HB, HB, VM, VM, VM, HB, VM, VM],
        out_specs=(VM, VM),
        scratch_shapes=[
            pltpu.VMEM(w_qkv.shape, BF16),
            pltpu.VMEM((T, width, D), BF16),
            pltpu.VMEM(head_w1.shape, BF16),
            pltpu.VMEM((T, block, D), BF16),
            pltpu.VMEM((T, block, 3 * width), F32),
            pltpu.VMEM((HL, half, 128), BF16),
            pltpu.VMEM((HL, rows, 128), BF16),
            pltpu.VMEM((HL, half, 128), BF16),
            pltpu.VMEM((S, rows, 128), BF16),
            pltpu.VMEM((2 * HL, half, 128), BF16),
            pltpu.VMEM((per * rows, 128), BF16),
            pltpu.VMEM((2 * HL, half, 128), F32),
            pltpu.VMEM((2 * HL, half, 1), F32),
            pltpu.VMEM((N, 80, 128), BF16),
            pltpu.VMEM((N, 80, 128), BF16),
            pltpu.VMEM((block, D), BF16),
            pltpu.VMEM((T, block, D), BF16),
            pltpu.VMEM((3, 32, block), F32),
            pltpu.VMEM((T, 32, block), F32),
            dma((3,)), dma((3,)), dma((3,)), dma((3,)),
            dma((HL,)), dma((HL,)), dma((HL,)), dma((HL,)),
            dma((HL, G)), dma((HL, G)), dma((HL, T)), dma((HL, T)),
            dma((3,)), dma((3,)), dma((3,)), dma((3,)), dma((6,)),
        ],
        compiler_params=pltpu.CompilerParams(
            collective_id=0, has_side_effects=True, vmem_limit_bytes=48 * 2**20
        ),
        name="sublayer",
    )(
        tokens, shift_scale, w_qkv, w_out, branch_gate.reshape(1, D), final_gain.reshape(1, D),
        type_ids.reshape(1, block), head_w1, head_b1, jnp.transpose(head_w2, (0, 2, 1)),
    )
    return (updated, heads.T)


def solution(mesh):
    in_specs = (
        P(("seq", "type"), None),
        P(),
        P(),
        P(),
        P(None, None, "type"),
        P("type", None),
        P(("seq", "type"), None),
        P("type", None, None),
        P("type", None),
        P("type", None, None),
    )
    out_specs = (P(("seq", "type"), None), P(("seq", "type"), None))
    return jax.shard_map(
        functools.partial(body, mesh.shape["seq"], mesh.shape["type"]),
        mesh=mesh, in_specs=in_specs, out_specs=out_specs, check_vma=False,
    )
```

```python
import functools

import jax
import jax.numpy as jnp
from jax import lax
from jax.experimental import pallas as pl
from jax.experimental.pallas import tpu as pltpu
from jax.sharding import PartitionSpec as P

HD = 64
MESH = pl.DeviceIdType.MESH
F32 = jnp.float32
BF16 = jnp.bfloat16


def rms_normalize(values):
    squares = jnp.mean(values * values, axis=-1, keepdims=True)
    return values * lax.rsqrt(squares + 1e-06)


def greet(peers):
    barrier = pltpu.get_barrier_semaphore()
    for peer in peers:
        pl.semaphore_signal(barrier, inc=1, device_id=peer, device_id_type=MESH)
    pl.semaphore_wait(barrier, len(peers))


def remote(src, dst, send, recv, peer):
    return pltpu.make_async_remote_copy(
        src_ref=src, dst_ref=dst, send_sem=send, recv_sem=recv, device_id=peer, device_id_type=MESH
    )


def partners(t):
    core = t + 1 - 2 * (t % 2)
    across = (t + 2) % 4
    diag = core + 2 - 4 * (core // 2)
    return core, across, diag


def kernel(
    S, HL, T,
    tok_h, ss_h, wqkv, wout, gate_h, gain_h, kinds_h, w1, b1_h, w2_h,
    upd_out, head_out,
    tok, ss, gate, gain, kinds, b1, w2, i_s,
    wq, wf, w1v, mod, proj, qsend, kvsend, qrecv, kv, qpad, vv, numer, top,
    asend, arecv, att, fin, rsend, rrecv,
    m_s, m_r, w_s, w_r, q_s, q_r, k_s, k_r, f_s, f_r, a_s, a_r, n_s, n_r, r_s, r_r, l_s,
):
    G = S // HL
    N = HL * T
    s = lax.axis_index("seq")
    t = lax.axis_index("type")
    h0, g = s // G, s % G
    core, across, diag = partners(t)
    zs = [((h0 + d) % HL) * G + g for d in range(HL)]
    groups = [h0 * G + (g + e) % G for e in range(G)]
    back = [(h0 + HL - d) % HL for d in range(HL)]
    block = tok_h.shape[0]
    rows = T * block
    half = rows // 2

    loads = [
        pltpu.make_async_copy(a, b, i_s.at[i])
        for i, (a, b) in enumerate(
            (
                (tok_h, tok), (ss_h, ss), (gate_h, gate), (gain_h, gain), (kinds_h, kinds),
                (b1_h, b1), (w2_h, w2),
            )
        )
    ]
    for c in loads:
        c.start()
    load_q = pltpu.make_async_copy(wqkv, wq, l_s.at[0])
    load_q.start()
    load_o = pltpu.make_async_copy(wout, wf.at[t], l_s.at[1])
    load_o.start()
    load_1 = pltpu.make_async_copy(w1, w1v, l_s.at[2])
    load_1.start()

    def device(h, tt):
        return (h * G + g, tt)

    greet(
        [
            device((h0 + d) % HL, (t + c) % T)
            for d in range(HL) for c in range(T) if d or c
        ]
        + [(groups[e], t) for e in range(1, G)]
    )
    sends = []
    mid = tok.shape[1] // 2

    def keep(ref, value):
        ref[t, 0] = value[:, :mid]
        ref[t, 1] = value[:, mid:]

    def whole(ref, i):
        return jnp.concatenate([ref[i, 0], ref[i, 1]], axis=-1)

    for c in loads:
        c.wait()
    x = tok[...].astype(F32)
    keep(mod, (rms_normalize(x) * (1.0 + ss[1:2]) + ss[0:1]).astype(BF16))
    def send(src, dst, a, b, peer):
        c = remote(src, dst, a, b, peer)
        c.start()
        sends.append(c)

    def arrive(slot, a, b):
        remote(slot, slot, a, b, (s, core)).wait_recv()

    for c in range(2):
        send(mod.at[t, c], mod.at[t, c], m_s.at[1, c], m_r.at[1, c], (s, across))
    for c in range(2):
        send(mod.at[t, c], mod.at[t, c], m_s.at[0, c], m_r.at[0, c], (s, core))

    def project(i):
        value = whole(mod, i)
        for which in range(3):
            proj[i, :, which * 256 : which * 256 + 256] = jnp.dot(
                value, wq[which], preferred_element_type=F32
            )

    def ship(p):
        y = (t // 2 + p) % 2
        for h in range(HL):
            lo = proj[2 * y, :, h * HD : h * HD + HD]
            hi = proj[2 * y + 1, :, h * HD : h * HD + HD]
            qsend[h, y] = jnp.concatenate([lo, hi], axis=-1).astype(BF16)
            k = proj[pl.ds(2 * y, 2), :, 256 + h * HD : 256 + h * HD + HD].reshape(half, HD)
            v = proj[pl.ds(2 * y, 2), :, 512 + h * HD : 512 + h * HD + HD].reshape(half, HD)
            kvsend[h, y] = jnp.concatenate([k, v], axis=-1).astype(BF16)
        for e in range(1, G):
            send(kvsend.at[h0, y], kv.at[s, y], f_s.at[0, e, p], f_r.at[0, e, p], (groups[e], t))
        for d in range(1, HL):
            hp = (h0 + d) % HL
            send(qsend.at[hp, y], qrecv.at[h0, y], q_s.at[d, p], q_r.at[d, p], (zs[d], t))
            send(kvsend.at[hp, y], kv.at[s, y], k_s.at[d, p], k_r.at[d, p], (zs[d], t))

    def pass_on(d, p):
        y = (t // 2 + p) % 2
        slot = kv.at[back[d] * G + g, y]
        arrive(slot, k_s.at[d, p], k_r.at[d, p])
        for e in range(1, G):
            send(slot, slot, f_s.at[d, e, p], f_r.at[d, e, p], (groups[e], t))

    load_q.wait()
    project(t)
    for c in range(2):
        arrive(mod.at[core, c], m_s.at[0, c], m_r.at[0, c])
    project(core)
    ship(0)
    for c in range(2):
        slot = mod.at[across, c]
        arrive(slot, m_s.at[1, c], m_r.at[1, c])
        send(slot, slot, m_s.at[2, c], m_r.at[2, c], (s, core))
    send(wout, wf.at[t], w_s.at[1], w_r.at[1], (s, across))
    project(across)
    for c in range(2):
        arrive(mod.at[diag, c], m_s.at[2, c], m_r.at[2, c])
    project(diag)

    ship(1)
    own_q = pltpu.make_async_copy(qsend.at[h0], qrecv.at[h0], l_s.at[3])
    own_q.start()
    own_kv = pltpu.make_async_copy(kvsend.at[h0], kv.at[s], l_s.at[4])
    own_kv.start()
    send(wout, wf.at[t], w_s.at[0], w_r.at[0], (s, core))

    def unpack(h):
        value = qrecv[h].astype(F32).reshape(half, 128).astype(BF16)
        zeros = jnp.zeros((half, HD), BF16)
        qpad[h * 2] = jnp.concatenate([value[:, :HD], zeros], axis=-1)
        qpad[h * 2 + 1] = jnp.concatenate([value[:, HD:], zeros], axis=-1)

    own_q.wait()
    unpack(h0)
    for d in range(1, HL):
        for p in range(2):
            arrive(qrecv.at[back[d], (t // 2 + p) % 2], q_s.at[d, p], q_r.at[d, p])
        unpack(back[d])
    own_kv.wait()

    factor = HD ** (-0.5) * 1.4426950408889634
    chunks = max(G // 2, 1)
    per = G // chunks

    def keys_of(d, j):
        return kv[pl.ds(back[d] * G + j * per, per)].reshape(per * rows, 128)

    def values(d, j):
        value = keys_of(d, j)
        lane = lax.broadcasted_iota(jnp.int32, value.shape, 1)
        vv[...] = jnp.where(lane < HD, jnp.ones_like(value), value)

    def pair(d, j, h, first):
        kc = keys_of(d, j)
        scores = [
            lax.dot_general(
                qpad[h * 2 + i], kc, (((1,), (1,)), ((), ())), preferred_element_type=F32
            )
            for i in range(2)
        ]
        for i in range(2):
            sc = scores[i]
            m = jnp.max(sc, axis=-1, keepdims=True)
            if not first:
                old = top[h * 2 + i]
                m = jnp.maximum(m, old)
            p = jnp.exp2((sc - m) * factor).astype(BF16)
            o = jnp.dot(p, vv[...], preferred_element_type=F32)
            if not first:
                o = o + numer[h * 2 + i] * jnp.exp2((old - m) * factor)
            numer[h * 2 + i] = o
            top[h * 2 + i] = m

    def absorb(d, first_h, count):
        first = d == 0 and chunks == 1

        def over_chunks(j, carry):
            values(d, j)

            def over(i, inner):
                pair(d, j, (first_h + i) % HL, first)
                return inner

            lax.fori_loop(0, count, over, 0)
            return carry

        if chunks == 1:
            over_chunks(0, 0)
        else:
            lax.fori_loop(0, chunks, over_chunks, 0)

    if chunks > 1:
        numer[...] = jnp.zeros_like(numer)
        top[...] = jnp.full_like(top, -1e30)

    def group_arrives(d):
        for e in range(1, G):
            for p in range(2):
                slot = kv.at[back[d] * G + (g + G - e) % G, (t // 2 + p) % 2]
                arrive(slot, f_s.at[d, e, p], f_r.at[d, e, p])

    def emit(h):
        parts = []
        for i in range(2):
            o = numer[h * 2 + i]
            a = o[:, HD:] / o[:, :HD]
            for j in range(2):
                b = a[j * block : (j + 1) * block]
                asend[h * T + j * 2 + i] = jnp.concatenate(
                    [b[0:80], b[block - 80 : block]], axis=-1
                ).astype(BF16)

    mine = t * HL + h0
    group_arrives(0)
    pass_on(1, 0)
    for d in range(HL - 1):
        absorb(d, h0, HL // 2)
        pass_on(d + 1, 1)
        if d == 0:
            arrive(wf.at[across], w_s.at[1], w_r.at[1])
            send(wf.at[across], wf.at[across], w_s.at[2], w_r.at[2], (s, core))
        absorb(d, h0 + HL // 2, HL // 2)
        if d + 2 < HL:
            pass_on(d + 2, 0)
        group_arrives(d + 1)
    for i in range(HL):
        d = (i + 1) % HL
        h = (h0 + d) % HL
        absorb(HL - 1, h, 1)
        emit(h)
        for c in range(T):
            if d or c:
                tt = (t + c) % T
                send(
                    asend.at[h * T + tt], arecv.at[mine], a_s.at[d, c], a_r.at[d, c],
                    device(h, tt),
                )
    own_a = pltpu.make_async_copy(asend.at[h0 * T + t], arecv.at[mine], l_s.at[5])
    own_a.start()
    arrive(wf.at[core], w_s.at[0], w_r.at[0])
    arrive(wf.at[diag], w_s.at[2], w_r.at[2])
    load_o.wait()
    own_a.wait()
    for i in range(HL):
        d = (i + 1) % HL
        for c in range(T):
            if d or c:
                arrive(arecv.at[((t + T - c) % T) * HL + back[d]], a_s.at[d, c], a_r.at[d, c])
    for j in range(N // 2):
        both = []
        for i in (2 * j, 2 * j + 1):
            r = arecv[i].astype(F32)
            both.append(jnp.concatenate([r[:, :HD], r[160 - block : 80, HD:]], axis=0))
        att[:, 128 * j : 128 * j + 128] = jnp.concatenate(both, axis=-1).astype(BF16)
    mixed = jnp.dot(
        att[...], wf[...].reshape(N * HD, tok.shape[1]), preferred_element_type=F32
    )
    updated = (tok[...].astype(F32) + gate[...] * mixed).astype(BF16)
    upd_out[...] = updated
    keep(fin, (rms_normalize(updated.astype(F32)) * gain[...]).astype(BF16))
    for c in range(2):
        send(fin.at[t, c], fin.at[t, c], n_s.at[1, c], n_r.at[1, c], (s, across))
    for c in range(2):
        send(fin.at[t, c], fin.at[t, c], n_s.at[0, c], n_r.at[0, c], (s, core))

    def heads(i, dst):
        f = whole(fin, i)
        for k in range(2):
            hid = jnp.dot(f, w1v[k], preferred_element_type=F32) + b1[k : k + 1].astype(F32)
            hid = jax.nn.gelu(hid).astype(BF16)
            dst[k * 16 : k * 16 + 16, :] = lax.dot_general(
                w2[k], hid, (((1,), (1,)), ((), ())), preferred_element_type=F32
            )

    load_1.wait()
    heads(t, rrecv.at[t])
    for c in range(2):
        arrive(fin.at[core, c], n_s.at[0, c], n_r.at[0, c])
    heads(core, rsend.at[0])
    send(rsend.at[0], rrecv.at[t], r_s.at[0], r_r.at[0], (s, core))
    for c in range(2):
        slot = fin.at[across, c]
        arrive(slot, n_s.at[1, c], n_r.at[1, c])
        send(slot, slot, n_s.at[2, c], n_r.at[2, c], (s, core))
    heads(across, rsend.at[1])
    send(rsend.at[1], rrecv.at[t], r_s.at[1], r_r.at[1], (s, across))
    for c in range(2):
        arrive(fin.at[diag, c], n_s.at[2, c], n_r.at[2, c])
    heads(diag, rsend.at[2])
    send(rsend.at[2], rrecv.at[t], r_s.at[2], r_r.at[2], (s, diag))
    for i, peer in enumerate((core, across, diag)):
        arrive(rrecv.at[peer], r_s.at[i], r_r.at[i])
    kind = kinds[...]
    total = jnp.zeros((16, block), F32)
    for owner in range(T):
        for k in range(2):
            total = jnp.where(kind == 2 * owner + k, rrecv[owner, k * 16 : k * 16 + 16, :], total)
    head_out[...] = total
    for c in sends:
        c.wait_send()


VM = pl.BlockSpec(memory_space=pltpu.VMEM)
HB = pl.BlockSpec(memory_space=pltpu.HBM)


def body(
    S, T,
    tokens, shift_scale, branch_gate, final_gain, w_qkv, w_out, type_ids, head_w1, head_b1, head_w2
):
    block, D = tokens.shape
    width = w_qkv.shape[2]
    HL = width // HD
    G = S // HL
    N = HL * T
    rows = block * T
    half = rows // 2
    per = min(G, 2)
    dma = pltpu.SemaphoreType.DMA
    updated, heads = pl.pallas_call(
        functools.partial(kernel, S, HL, T),
        out_shape=(
            jax.ShapeDtypeStruct((block, D), BF16),
            jax.ShapeDtypeStruct((16, block), F32),
        ),
        in_specs=[HB] * 10,
        out_specs=(VM, VM),
        scratch_shapes=[
            pltpu.VMEM((block, D), BF16),
            pltpu.VMEM((2, D), F32),
            pltpu.VMEM((1, D), F32),
            pltpu.VMEM((1, D), F32),
            pltpu.VMEM((1, block), jnp.int32),
            pltpu.VMEM(head_b1.shape, BF16),
            pltpu.VMEM((head_w2.shape[0], head_w2.shape[2], head_w2.shape[1]), BF16),
            dma((7,)),
            pltpu.VMEM(w_qkv.shape, BF16),
            pltpu.VMEM((T, width, D), BF16),
            pltpu.VMEM(head_w1.shape, BF16),
            pltpu.VMEM((T, 2, block, D // 2), BF16),
            pltpu.VMEM((T, block, 3 * width), F32),
            pltpu.VMEM((HL, 2, block, 128), BF16),
            pltpu.VMEM((HL, 2, half, 128), BF16),
            pltpu.VMEM((HL, 2, block, 128), BF16),
            pltpu.VMEM((S, 2, half, 128), BF16),
            pltpu.VMEM((2 * HL, half, 128), BF16),
            pltpu.VMEM((per * rows, 128), BF16),
            pltpu.VMEM((2 * HL, half, 128), F32),
            pltpu.VMEM((2 * HL, half, 1), F32),
            pltpu.VMEM((N, 80, 128), BF16),
            pltpu.VMEM((N, 80, 128), BF16),
            pltpu.VMEM((block, D), BF16),
            pltpu.VMEM((T, 2, block, D // 2), BF16),
            pltpu.VMEM((3, 32, block), F32),
            pltpu.VMEM((T, 32, block), F32),
            dma((3, 2)), dma((3, 2)), dma((3,)), dma((3,)),
            dma((HL, 2)), dma((HL, 2)), dma((HL, 2)), dma((HL, 2)),
            dma((HL, G, 2)), dma((HL, G, 2)), dma((HL, T)), dma((HL, T)),
            dma((3, 2)), dma((3, 2)), dma((3,)), dma((3,)), dma((6,)),
        ],
        compiler_params=pltpu.CompilerParams(
            collective_id=0, has_side_effects=True, vmem_limit_bytes=63 * 2**20
        ),
        name="sublayer",
    )(
        tokens, shift_scale, w_qkv, w_out, branch_gate.reshape(1, D), final_gain.reshape(1, D),
        type_ids.reshape(1, block), head_w1, head_b1, jnp.transpose(head_w2, (0, 2, 1)),
    )
    return (updated, heads.T)


def solution(mesh):
    in_specs = (
        P(("seq", "type"), None),
        P(),
        P(),
        P(),
        P(None, None, "type"),
        P("type", None),
        P(("seq", "type"), None),
        P("type", None, None),
        P("type", None),
        P("type", None, None),
    )
    out_specs = (P(("seq", "type"), None), P(("seq", "type"), None))
    return jax.shard_map(
        functools.partial(body, mesh.shape["seq"], mesh.shape["type"]),
        mesh=mesh, in_specs=in_specs, out_specs=out_specs, check_vma=False,
    )
```
